256 devices in a mesh: dp: 32 (over x, y, core), tensor: 8 (over z).
Axes of the slice: x: 4, y: 4, z: 8, core: 2. Of those that a mesh axis runs over, the one named last changes fastest.
Arguments:
- queries: bfloat16 [20480, 5120], P('dp', 'tensor'), may hold values from -12 to 12
- key_states: bfloat16 [20480, 1024], P('dp', 'tensor'), may hold values from -6 to 6
- window_values: bfloat16 [20480, 1024], P('dp', 'tensor'), may hold values from -6 to 6
- doc_lengths: int32 [64], replicated, may hold values from 0 to 7, as said below
- doc_owners: int32 [64], replicated, may hold values from 0 to 31, as said below
- out_weight: bfloat16 [5120, 5120], P('tensor', 'dp'), may hold values from -0.078125 to 0.078125
- grad_context: bfloat16 [28672, 5120], P('dp', 'tensor'), may hold values from -6 to 6
Outputs:
- projected: bfloat16 [28672, 5120], P('dp', 'tensor')
- grad_queries: bfloat16 [28672, 5120], P('dp', 'tensor')
- key_gradient: bfloat16 [28672, 1024], P('dp', 'tensor')
- value_gradient: bfloat16 [28672, 1024], P('dp', 'tensor')
The draws below stay inside these ranges and needn't reach their ends.
Inputs may be any that keep to these rules, and one draw needn't show every extreme that they name: `doc_owners`: owners never fall along the documents; every shard owns one to three documents; shard s's range starts within 1 block of block s * 5 (both ends reached), so one range holds at most 7 blocks, a bound reached in every draw. `doc_lengths`: lengths may be zero; they sum to 160.
All inputs are finite; a program needn't handle non-finite values.
Results may differ from the reference program's by a relative error of at most 0.03.
Values may be sent and summed in bfloat16 or wider, within the bound.
No kernel may reach another device: no remote copies, remote signals or barrier semaphores. Data moves between devices by JAX's collectives and lax.ppermute only.
A program may use at most 128 MiB of HBM per device.

```python
import jax
import jax.numpy as jnp
from jax import lax

D = 5120
HQ = 40
KEY_VALUE_HEADS = 8
HEAD_SIZE = 128
BLOCK = 128
RIM = 1
NB = 5
CAP = 7
WINDOW_TOKENS = 20480
ROWS = 28672
N_DP = 32
N_TENSOR = 8


def layout_tables(key):
    shards = N_DP
    key_rim, key_count, key_first, key_second = jax.random.split(key, 4)
    shifts = jax.random.randint(key_rim, (shards + 1,), -RIM, RIM + 1)
    shifts = shifts.at[0].set(0).at[shards].set(0).at[1].set(-RIM).at[2].set(RIM)
    bounds = jnp.arange(shards + 1, dtype=jnp.int32) * NB + shifts
    spans = bounds[1:] - bounds[:-1]
    halves = jax.random.randint(key_count, ((shards + 1) // 2,), 1, 4)
    halves = halves.at[0].set(3)
    counts = jnp.stack([halves, 4 - halves], axis=1).reshape(-1)[:shards]
    if shards % 2 == 1:
        counts = counts.at[shards - 1].set(2)
    doc_owners = jnp.repeat(jnp.arange(shards, dtype=jnp.int32), counts, total_repeat_length=2 * shards)
    firsts = jnp.cumsum(counts) - counts
    within = jnp.arange(2 * shards, dtype=jnp.int32) - firsts[doc_owners]
    first_cut = jax.random.randint(key_first, (shards,), 0, spans + 1)
    second_cut = jax.random.randint(key_second, (shards,), 0, spans - first_cut + 1)
    own_count = counts[doc_owners]
    own_span = spans[doc_owners]
    cut_one = first_cut[doc_owners]
    cut_two = second_cut[doc_owners]
    remainder = own_span - jnp.where(within >= 1, cut_one, 0) - jnp.where(within >= 2, cut_two, 0)
    doc_lengths = jnp.where(within == own_count - 1, remainder, jnp.where(within == 0, cut_one, cut_two))
    return (doc_lengths.astype(jnp.int32), doc_owners.astype(jnp.int32))


def draw_doc_lengths(key, part):
    return layout_tables(key)[0]


def draw_doc_owners(key, part):
    return layout_tables(key)[1]


def draw_queries(key, part):
    key = jax.random.fold_in(key, 3)
    base_key = jax.random.fold_in(key, 0)
    value_heads = jax.random.truncated_normal(base_key, -6.0, 6.0, (WINDOW_TOKENS, HQ * HEAD_SIZE), jnp.float32)
    return value_heads.astype(jnp.bfloat16)


def draw_key_states(key, part):
    key = jax.random.fold_in(key, 4)
    value_heads = jax.random.truncated_normal(key, -6.0, 6.0, (WINDOW_TOKENS, KEY_VALUE_HEADS * HEAD_SIZE), jnp.float32)
    return value_heads.astype(jnp.bfloat16)


def levels(rng, extent, pieces, least, high):
    def one(position, blocks):
        draws = jax.random.uniform(jax.random.fold_in(jax.random.fold_in(rng, 6), position), (blocks,), jnp.float32, least / len(pieces), high / len(pieces))
        return jnp.repeat(jnp.exp(draws), extent[position] // blocks).reshape((-1,) + (1,) * (len(extent) - position - 1))

    level = one(*pieces[0])
    for cut in pieces[1:]:
        level = level * one(*cut)
    return level


def bell_draw(own_key, dims, width, limit, cuts=(), held_as=jnp.bfloat16):
    values = width * jax.random.normal(own_key, dims, jnp.float32)
    if cuts:
        values = values * levels(own_key, dims, cuts, -0.22, 0.18)
    return jnp.clip(values, -limit, limit).astype(held_as)


def setup_inputs(seed: int = 0) -> dict:
    key_of = jax.random.split(jax.random.key(seed), 8)
    queries = draw_queries(jax.random.fold_in(key_of[7], 71), 0)
    key_states = draw_key_states(jax.random.fold_in(key_of[7], 71), 0)
    window_values = bell_draw(key_of[2], (WINDOW_TOKENS, KEY_VALUE_HEADS * HEAD_SIZE), 1.0, 6.0, ((0, 32), (1, 8)))
    doc_lengths = draw_doc_lengths(jax.random.fold_in(key_of[7], 71), 0)
    doc_owners = draw_doc_owners(jax.random.fold_in(key_of[7], 71), 0)
    out_weight = bell_draw(key_of[5], (HQ * HEAD_SIZE, D), (HQ * HEAD_SIZE) ** -0.5, 0.078125, ((0, 8), (1, 32)))
    grad_context = bell_draw(key_of[6], (ROWS, HQ * HEAD_SIZE), 1.0, 6.0, ((0, 32), (1, 8)))
    return dict(queries=queries, key_states=key_states, window_values=window_values, doc_lengths=doc_lengths, doc_owners=doc_owners, out_weight=out_weight, grad_context=grad_context)


def attend(query_rows, key_rows, value_rows, grad_rows, query_doc, query_pos, key_doc, key_pos):
    count_q = query_rows.shape[0]
    count_k = key_rows.shape[0]
    kv_heads = key_rows.shape[1] // HEAD_SIZE
    per_group = query_rows.shape[1] // key_rows.shape[1]
    factor = HEAD_SIZE ** -0.5
    split_q = query_rows.astype(jnp.float32).reshape(count_q, kv_heads, per_group, HEAD_SIZE)
    split_k = key_rows.astype(jnp.float32).reshape(count_k, kv_heads, HEAD_SIZE)
    split_v = value_rows.astype(jnp.float32).reshape(count_k, kv_heads, HEAD_SIZE)
    highest = lax.Precision.HIGHEST
    scores = jnp.einsum("qhgd,khd->hgqk", split_q, split_k, precision=highest) * factor
    allowed = (query_doc[:, None] == key_doc[None, :]) & (key_pos[None, :] <= query_pos[:, None])
    scores = jnp.where(allowed[None, None], scores, -1e30)
    top_score = jnp.max(scores, axis=-1, keepdims=True)
    weights = jnp.exp(scores - top_score)
    probs = weights / jnp.sum(weights, axis=-1, keepdims=True)
    prob_low = probs.astype(jnp.bfloat16).astype(jnp.float32)
    live_rows = query_doc >= 0
    context = jnp.einsum("hgqk,khd->qhgd", prob_low, split_v, precision=highest)
    context = jnp.where(live_rows[:, None, None, None], context, 0.0)
    context_low = context.astype(jnp.bfloat16)
    grad_in = jnp.where(live_rows[:, None], grad_rows, jnp.zeros_like(grad_rows))
    grad_in = grad_in.astype(jnp.float32).reshape(count_q, kv_heads, per_group, HEAD_SIZE)
    delta = jnp.sum(grad_in * context_low.astype(jnp.float32), axis=-1)
    grad_prob = jnp.einsum("qhgd,khd->hgqk", grad_in, split_v, precision=highest)
    grad_score = probs * (grad_prob - jnp.transpose(delta, (1, 2, 0))[..., None])
    score_low = grad_score.astype(jnp.bfloat16).astype(jnp.float32)
    grad_v = jnp.einsum("hgqk,qhgd->khd", prob_low, grad_in, precision=highest)
    grad_q = jnp.einsum("hgqk,khd->qhgd", score_low, split_k, precision=highest) * factor
    grad_k = jnp.einsum("hgqk,qhgd->khd", score_low, split_q, precision=highest) * factor
    return (context_low.reshape(count_q, -1), grad_q.reshape(count_q, -1),
            grad_k.reshape(count_k, -1), grad_v.reshape(count_k, -1))


def doc_tables(doc_lengths, doc_owners, shard, row_indices):
    ends = jnp.cumsum(doc_lengths).astype(jnp.int32)
    first = jnp.sum(jnp.where(doc_owners < shard, doc_lengths, 0)).astype(jnp.int32)
    last = jnp.sum(jnp.where(doc_owners <= shard, doc_lengths, 0)).astype(jnp.int32)
    positions = first * BLOCK + jnp.arange(row_indices, dtype=jnp.int32)
    block_ids = positions // BLOCK
    live_rows = positions < last * BLOCK
    doc_ids = jnp.sum((ends[None, :] <= block_ids[:, None]).astype(jnp.int32), axis=1).astype(jnp.int32)
    query_doc = jnp.where(live_rows, doc_ids, -1).astype(jnp.int32)
    key_doc = jnp.where(live_rows, doc_ids, -2).astype(jnp.int32)
    return first, positions, query_doc, key_doc


def reference(queries, key_states, window_values, doc_lengths, doc_owners, out_weight, grad_context):
    row_indices = CAP * BLOCK

    def padded(source):
        return jnp.concatenate([source, jnp.zeros((row_indices, source.shape[1]), source.dtype)], axis=0)

    query_pad = padded(queries)
    key_pad = padded(key_states)
    value_pad = padded(window_values)
    grad_slots = grad_context.reshape(N_DP, row_indices, HQ * HEAD_SIZE)
    columns = HQ * HEAD_SIZE // N_TENSOR

    def one_shard(inputs):
        shard, grad_rows = inputs
        first, positions, query_doc, key_doc = doc_tables(doc_lengths, doc_owners, shard, row_indices)
        start = (first * BLOCK).astype(jnp.int32)
        query_rows = lax.dynamic_slice_in_dim(query_pad, start, row_indices, 0)
        key_rows = lax.dynamic_slice_in_dim(key_pad, start, row_indices, 0)
        value_rows = lax.dynamic_slice_in_dim(value_pad, start, row_indices, 0)
        context, grad_q, grad_k, grad_v = attend(query_rows, key_rows, value_rows, grad_rows,
                                                 query_doc, positions, key_doc, positions)
        total = jnp.zeros((row_indices, D), jnp.float32)
        for group_id in range(N_TENSOR):
            partial_rows = jnp.dot(context[:, group_id * columns:(group_id + 1) * columns],
                                   out_weight[group_id * columns:(group_id + 1) * columns],
                                   preferred_element_type=jnp.float32)
            rounded = lax.optimization_barrier(partial_rows.astype(jnp.bfloat16))
            total = total + rounded.astype(jnp.float32)
        return (total.astype(jnp.bfloat16), grad_q.astype(jnp.bfloat16),
                grad_k.astype(jnp.bfloat16), grad_v.astype(jnp.bfloat16))

    output_rows = lax.map(one_shard, (jnp.arange(N_DP, dtype=jnp.int32), grad_slots))
    projected = output_rows[0].reshape(N_DP * row_indices, D)
    grad_queries = output_rows[1].reshape(N_DP * row_indices, HQ * HEAD_SIZE)
    key_gradient = output_rows[2].reshape(N_DP * row_indices, KEY_VALUE_HEADS * HEAD_SIZE)
    value_gradient = output_rows[3].reshape(N_DP * row_indices, KEY_VALUE_HEADS * HEAD_SIZE)
    return (projected, grad_queries, key_gradient, value_gradient)
```

```python
import functools

import jax
import jax.numpy as jnp
from jax import lax
from jax.experimental import pallas as pl
from jax.experimental.pallas import tpu as pltpu
from jax.sharding import PartitionSpec as P

HEAD = 128
BLOCK = 128
OWN = 5
WIDE = 7
HEADS = 5
Q_COLS = HEADS * HEAD
EDGE_COLS = Q_COLS + 2 * HEAD
FACTOR = HEAD ** (-0.5)
EXP_FACTOR = FACTOR * 1.4426950408889634
MASKED = -1e30
NT = (((1,), (1,)), ((), ()))
TN = (((0,), (0,)), ((), ()))

KEY_START = 0
LIVE = WIDE
OFFSET = 2 * WIDE


def rows_of(block, count=1):
    return pl.ds(block * BLOCK, count * BLOCK)


def dot(a, b, dims=None):
    if dims is None:
        return jnp.dot(a, b, preferred_element_type=jnp.float32)
    return lax.dot_general(a, b, dims, preferred_element_type=jnp.float32)


def fill_wide(wide, own, before, after, column):
    cols = slice(column, column + HEAD)
    wide[0:BLOCK] = before[:, cols]
    wide[BLOCK:BLOCK * (OWN + 1)] = own[...]
    wide[BLOCK * (OWN + 1):] = after[:, cols]


def query_block(own, before, after, block, head):
    cols = slice(head * HEAD, (head + 1) * HEAD)
    if block == 0:
        return before[:, cols]
    if block == WIDE - 1:
        return after[:, cols]
    return own[rows_of(block - 1), cols]


def forward_kernel(table, q, k, v, before, after, center, low, high, outer_low, outer_high, k_wide, v_wide):
    fill_wide(k_wide, k, before, after, Q_COLS)
    v_wide[:, HEAD:] = jnp.ones((WIDE * BLOCK, HEAD), jnp.bfloat16)
    v_wide[0:BLOCK, :HEAD] = before[:, Q_COLS + HEAD:]
    v_wide[BLOCK:BLOCK * (OWN + 1), :HEAD] = v[...]
    v_wide[BLOCK * (OWN + 1):, :HEAD] = after[:, Q_COLS + HEAD:]
    targets = [outer_low, low, center, center, center, high, outer_high]
    for block in (2, 3, 4, 0, 1, 5, 6):
        target = targets[block]
        base = (block - 2) if 2 <= block <= 4 else 0
        keys = (block + 1) * BLOCK

        def attend(block=block, target=target, base=base, keys=keys):
            row = lax.broadcasted_iota(jnp.int32, (BLOCK, keys), 0) + block * BLOCK
            col = lax.broadcasted_iota(jnp.int32, (BLOCK, keys), 1)
            allowed = (col <= row) & (col >= table[KEY_START + block] * BLOCK)
            bias = jnp.where(allowed, 0.0, MASKED)
            for head in range(HEADS):
                s = dot(query_block(q, before, after, block, head), k_wide[0:keys, :], NT)
                t = s * EXP_FACTOR + bias
                top = jnp.max(t, axis=1, keepdims=True)
                p = jnp.exp2(t - top).astype(jnp.bfloat16)
                both = dot(p, v_wide[0:keys, :])
                context = both[:, :HEAD] / both[:, HEAD:]
                target[rows_of(base), head * HEAD:(head + 1) * HEAD] = context.astype(jnp.bfloat16)

        if 2 <= block <= 4:
            attend()
        else:
            live = table[LIVE + block] != 0
            pl.when(live)(attend)

            @pl.when(jnp.logical_not(live))
            def _(target=target):
                target[...] = jnp.zeros_like(target)


def backward_kernel(
    table, q, k, v, before, after, grad, center, low, high, outer_low, outer_high,
    grad_q, grad_k, grad_v, k_wide, v_wide, k_turned, sum_k, sum_v, p_all, s_all,
):
    offset = table[OFFSET]
    fill_wide(k_wide, k, before, after, Q_COLS)
    fill_wide(v_wide, v, before, after, Q_COLS + HEAD)
    k_turned[...] = k_wide[...].T
    sum_k[...] = jnp.zeros_like(sum_k)
    sum_v[...] = jnp.zeros_like(sum_v)
    grad_q[...] = jnp.zeros_like(grad_q)
    sources = [outer_low, low, center, center, center, high, outer_high]
    for block in range(WIDE):
        source = sources[block]
        base = (block - 2) if 2 <= block <= 4 else 0
        keys = (block + 1) * BLOCK

        def attend(block=block, source=source, base=base, keys=keys):
            start = pl.multiple_of(jnp.clip(block - offset, 0, WIDE - 1) * BLOCK, BLOCK)
            slot = pl.ds(start, BLOCK)
            col = lax.broadcasted_iota(jnp.int32, (keys, BLOCK), 1) + block * BLOCK
            row = lax.broadcasted_iota(jnp.int32, (keys, BLOCK), 0)
            allowed = (row <= col) & (row >= table[KEY_START + block] * BLOCK)
            bias = jnp.where(allowed, 0.0, MASKED)
            queries = []
            grads = []
            for head in range(HEADS):
                cols = slice(head * HEAD, (head + 1) * HEAD)
                qh = query_block(q, before, after, block, head)
                gh = grad[slot, cols]
                queries.append(qh)
                grads.append(gh)
                s = dot(k_wide[0:keys, :], qh, NT)
                t = s * EXP_FACTOR + bias
                top = jnp.max(t, axis=0, keepdims=True)
                w = jnp.exp2(t - top)
                p = w * (1.0 / jnp.sum(w, axis=0, keepdims=True))
                p_all[0:keys, cols] = p.astype(jnp.bfloat16)
                c = source[rows_of(base), cols].astype(jnp.float32)
                delta = jnp.sum((gh.astype(jnp.float32) * c).T, axis=0, keepdims=True)
                gp = dot(v_wide[0:keys, :], gh, NT)
                ds = (p * (gp - delta)).astype(jnp.bfloat16)
                s_all[0:keys, cols] = ds
                gq = dot(k_turned[:, 0:keys], ds)
                grad_q[slot, cols] = (gq * FACTOR).T.astype(jnp.bfloat16)
            queries = jnp.concatenate(queries, axis=0)
            grads = jnp.concatenate(grads, axis=0)
            sum_v[0:keys, :] += dot(p_all[0:keys, :], grads)
            sum_k[0:keys, :] += dot(s_all[0:keys, :], queries)

        if 2 <= block <= 4:
            attend()
        else:
            pl.when(table[LIVE + block] != 0)(attend)
    shifted = pl.ds(pl.multiple_of(offset * BLOCK, BLOCK), WIDE * BLOCK)
    grad_k[...] = (sum_k[shifted, :] * FACTOR).astype(jnp.bfloat16)
    grad_v[...] = sum_v[shifted, :].astype(jnp.bfloat16)


VMEM = pl.BlockSpec(memory_space=pltpu.VMEM)
SMEM = pl.BlockSpec(memory_space=pltpu.SMEM)


def half(rows, cols=Q_COLS):
    return jax.ShapeDtypeStruct((rows, cols), jnp.bfloat16)


def forward(table, q, k, v, before, after):
    return pl.pallas_call(
        forward_kernel,
        out_shape=(half(3 * BLOCK), half(BLOCK), half(BLOCK), half(BLOCK), half(BLOCK)),
        in_specs=[SMEM] + [VMEM] * 5,
        out_specs=[VMEM] * 5,
        scratch_shapes=[
            pltpu.VMEM((WIDE * BLOCK, HEAD), jnp.bfloat16),
            pltpu.VMEM((WIDE * BLOCK, 2 * HEAD), jnp.bfloat16),
        ],
        compiler_params=pltpu.CompilerParams(vmem_limit_bytes=24 * 1024 * 1024),
        cost_estimate=pl.CostEstimate(flops=4_000_000_000, bytes_accessed=3_000_000, transcendentals=2_300_000),
        name="forward",
    )(table, q, k, v, before, after)


def backward(table, q, k, v, before, after, grad, contexts):
    return pl.pallas_call(
        backward_kernel,
        out_shape=(half(WIDE * BLOCK), half(WIDE * BLOCK, HEAD), half(WIDE * BLOCK, HEAD)),
        in_specs=[SMEM] + [VMEM] * 11,
        out_specs=[VMEM] * 3,
        scratch_shapes=[
            pltpu.VMEM((WIDE * BLOCK, HEAD), jnp.bfloat16),
            pltpu.VMEM((WIDE * BLOCK, HEAD), jnp.bfloat16),
            pltpu.VMEM((HEAD, WIDE * BLOCK), jnp.bfloat16),
            pltpu.VMEM(((WIDE + 2) * BLOCK, HEAD), jnp.float32),
            pltpu.VMEM(((WIDE + 2) * BLOCK, HEAD), jnp.float32),
            pltpu.VMEM((WIDE * BLOCK, Q_COLS), jnp.bfloat16),
            pltpu.VMEM((WIDE * BLOCK, Q_COLS), jnp.bfloat16),
        ],
        compiler_params=pltpu.CompilerParams(vmem_limit_bytes=32 * 1024 * 1024),
        cost_estimate=pl.CostEstimate(flops=8_000_000_000, bytes_accessed=5_000_000, transcendentals=2_300_000),
        name="backward",
    )(table, q, k, v, before, after, grad, *contexts)


def weight_block(weight, group):
    return jnp.concatenate([weight[group % 4, part, group // 4] for part in range(weight.shape[1])], axis=0)


def gather_kernel(groups, last_group, weight, *refs):
    count = len(groups)
    sources = refs[:2 * count]
    center_total, edge_total, last_weight = refs[2 * count:]
    last_weight[...] = weight_block(weight, last_group)
    for i, group in enumerate(groups):
        block = weight_block(weight, group)
        center = dot(sources[2 * i][...], block, NT)
        edge = dot(sources[2 * i + 1][...], block, NT)
        if i == 0:
            center_total[...] = center
            edge_total[...] = edge
        else:
            center_total[...] += center
            edge_total[...] += edge


def edge_kernel(weight, total, first, second, low, high):
    low[...] = (total[0:BLOCK, :] + dot(first[...], weight[...], NT)).astype(jnp.bfloat16)
    high[...] = (total[BLOCK:, :] + dot(second[...], weight[...], NT)).astype(jnp.bfloat16)


def finish_kernel(
    table, weight, total, first, second, outer_low, low, high, outer_high, projected, blocks, zeros, sems, zero_sems, center_sem
):
    offset = table[OFFSET]
    zeros[...] = jnp.zeros_like(zeros)
    outer = ((0, outer_low), (1, low), (WIDE - 2, high), (WIDE - 1, outer_high))

    def slot(block):
        return pl.ds(pl.multiple_of(block * BLOCK, BLOCK), BLOCK)

    def copy_outer(index, wait):
        block, source = outer[index]
        copy = pltpu.make_async_copy(
            source, projected.at[slot(jnp.clip(block - offset, 0, WIDE - 1)), :], sems.at[index]
        )
        pl.when(table[LIVE + block] != 0)(copy.wait if wait else copy.start)

    def copy_zeros(row, wait):
        copy = pltpu.make_async_copy(zeros, projected.at[slot(row), :], zero_sems.at[row])
        block = row + offset
        live = (block < WIDE) & (table[LIVE + jnp.minimum(block, WIDE - 1)] != 0)
        pl.when(jnp.logical_not(live))(copy.wait if wait else copy.start)

    for index in range(len(outer)):
        copy_outer(index, False)
    for row in range(WIDE):
        copy_zeros(row, False)
    rows = first.shape[0]
    blocks[0:rows, :] = (total[0:rows, :] + dot(first[...], weight[...], NT)).astype(jnp.bfloat16)
    blocks[rows:, :] = (total[rows:, :] + dot(second[...], weight[...], NT)).astype(jnp.bfloat16)
    start = pl.multiple_of(jnp.clip(2 - offset, 0, 2) * BLOCK, BLOCK)
    copy = pltpu.make_async_copy(blocks, projected.at[pl.ds(start, 2 * rows), :], center_sem)
    copy.start()
    for index in range(len(outer)):
        copy_outer(index, True)
    for row in range(WIDE):
        copy_zeros(row, True)
    copy.wait()


ANY = pl.BlockSpec(memory_space=pl.ANY)


def project_most(weight, arrived, last_group):
    groups = tuple(group for group, _, _ in arrived)
    pieces = [piece for _, center, edge in arrived for piece in (center, edge)]
    centers, edges = pieces[0].shape[0], pieces[1].shape[0]
    return pl.pallas_call(
        functools.partial(gather_kernel, groups, last_group),
        out_shape=(
            jax.ShapeDtypeStruct((centers, Q_COLS), jnp.float32),
            jax.ShapeDtypeStruct((edges, Q_COLS), jnp.float32),
            half(Q_COLS),
        ),
        in_specs=[VMEM] * (1 + len(pieces)),
        out_specs=[VMEM] * 3,
        compiler_params=pltpu.CompilerParams(vmem_limit_bytes=24 * 1024 * 1024),
        cost_estimate=pl.CostEstimate(flops=3_700_000_000, bytes_accessed=14_000_000, transcendentals=0),
        name="project_most",
    )(weight, *pieces)


def project_edge(weight, total, first, second):
    return pl.pallas_call(
        edge_kernel,
        out_shape=(half(BLOCK), half(BLOCK)),
        in_specs=[VMEM] * 4,
        out_specs=[VMEM] * 2,
        compiler_params=pltpu.CompilerParams(vmem_limit_bytes=16 * 1024 * 1024),
        cost_estimate=pl.CostEstimate(flops=210_000_000, bytes_accessed=2_200_000, transcendentals=0),
        name="project_edge",
    )(weight, total, first, second)


def finish(table, weight, total, first, second, blocks):
    return pl.pallas_call(
        finish_kernel,
        out_shape=half(WIDE * BLOCK),
        in_specs=[SMEM] + [VMEM] * 8,
        out_specs=ANY,
        scratch_shapes=[
            pltpu.VMEM((total.shape[0], Q_COLS), jnp.bfloat16),
            pltpu.VMEM((BLOCK, Q_COLS), jnp.bfloat16),
            pltpu.SemaphoreType.DMA((4,)),
            pltpu.SemaphoreType.DMA((WIDE,)),
            pltpu.SemaphoreType.DMA,
        ],
        compiler_params=pltpu.CompilerParams(vmem_limit_bytes=24 * 1024 * 1024),
        cost_estimate=pl.CostEstimate(flops=320_000_000, bytes_accessed=4_500_000, transcendentals=0),
        name="finish",
    )(table, weight, total, first, second, *blocks)


def tables(doc_lengths, doc_owners, device):
    count = doc_lengths.shape[0]
    order = jnp.arange(count, dtype=jnp.int32)
    ends = jnp.sum(jnp.where(order[None, :] <= order[:, None], doc_lengths[None, :], 0), axis=1)
    first = jnp.sum(jnp.where(doc_owners < device, doc_lengths, 0))
    last = jnp.sum(jnp.where(doc_owners <= device, doc_lengths, 0))
    origin = device * OWN - 1
    block = origin + jnp.arange(WIDE, dtype=jnp.int32)
    start = jnp.max(jnp.where(ends[None, :] <= block[:, None], ends[None, :], 0), axis=1)
    start = jnp.clip(start - origin, 0, WIDE - 1)
    live = ((block >= first) & (block < last)).astype(jnp.int32)
    offset = jnp.clip(first - origin, 0, 2)
    return jnp.concatenate([start, live, offset[None]]).astype(jnp.int32)


def body(queries, key_states, window_values, doc_lengths, doc_owners, out_weight, grad_context):
    dp, tensor = lax.axis_size("dp"), lax.axis_size("tensor")
    device = lax.axis_index("dp")
    up = [(i, i + 1) for i in range(dp - 1)]
    down = [(i + 1, i) for i in range(dp - 1)]
    right = [(i, (i + 1) % tensor) for i in range(tensor)]
    left = [((i + 1) % tensor, i) for i in range(tensor)]
    table = tables(doc_lengths, doc_owners, device)

    def edge(rows):
        return jnp.concatenate([queries[rows], key_states[rows], window_values[rows]], axis=1)

    before = lax.ppermute(edge(slice((OWN - 1) * BLOCK, OWN * BLOCK)), "dp", up)
    after = lax.ppermute(edge(slice(0, BLOCK)), "dp", down)

    per = dp // tensor
    turn = []
    for a in range(tensor):
        for b in range(tensor):
            g = (b - a) % tensor
            for e in range(per):
                turn.append(((per * a + e) * tensor + b, (((g % 4) * per + e) * 2 + g // 4) * tensor + a))
    piece = lax.ppermute(out_weight.T, ("dp", "tensor"), turn)

    contexts = forward(table, queries, key_states, window_values, before, after)
    center, low, high, outer_low, outer_high = contexts
    piece, _ = lax.optimization_barrier((piece, center))
    weight = lax.all_gather(piece, "dp", axis=0, tiled=True).reshape(4, per, 2, -1, Q_COLS)

    low_in = lax.ppermute(outer_high, "dp", up)
    high_in = lax.ppermute(outer_low, "dp", down)
    live = table[LIVE:LIVE + WIDE]
    edges = jnp.concatenate(
        [jnp.where(live[1] != 0, low, low_in), jnp.where(live[5] != 0, high, high_in)], axis=0
    )

    contexts = lax.optimization_barrier((contexts, edges))[0]
    grads = backward(table, queries, key_states, window_values, before, after, grad_context, contexts)

    hops = tensor // 2
    arrived = [(0, center, edges)]
    center_right = center_left = center
    edge_right = edge_left = edges
    for hop in range(1, hops):
        center_right = lax.ppermute(center_right, "tensor", right)
        center_left = lax.ppermute(center_left, "tensor", left)
        edge_right = lax.ppermute(edge_right, "tensor", right)
        edge_left = lax.ppermute(edge_left, "tensor", left)
        if hop == 1:
            center_right, center_left, grads = lax.optimization_barrier((center_right, center_left, grads))
        arrived.append((tensor - hop, center_right, edge_right))
        arrived.append((hop, center_left, edge_left))
    rows = center.shape[0] // 2
    edge_right = lax.ppermute(edge_right[:BLOCK], "tensor", right)
    edge_left = lax.ppermute(edge_left[BLOCK:], "tensor", left)
    center_right = lax.ppermute(center_right[:rows], "tensor", right)
    center_left = lax.ppermute(center_left[rows:], "tensor", left)

    center_total, edge_total, last_weight = project_most(weight, arrived, hops)
    low_out, high_out = project_edge(last_weight, edge_total, edge_right, edge_left)
    outer_low_out = lax.ppermute(high_out, "dp", up)
    outer_high_out = lax.ppermute(low_out, "dp", down)
    projected = finish(
        table, last_weight, center_total, center_right, center_left,
        (outer_low_out, low_out, high_out, outer_high_out),
    )
    return (projected, *grads)


def solution(mesh):
    placed = P("dp", "tensor")
    return jax.shard_map(
        body,
        mesh=mesh,
        in_specs=(placed, placed, placed, P(), P(), P("tensor", "dp"), placed),
        out_specs=(placed, placed, placed, placed),
        check_vma=False,
    )
```

```python
import functools

import jax
import jax.numpy as jnp
from jax import lax
from jax.experimental import pallas as pl
from jax.experimental.pallas import tpu as pltpu
from jax.sharding import PartitionSpec as P

HEAD = 128
BLOCK = 128
OWN = 5
WIDE = 7
HEADS = 5
Q_COLS = HEADS * HEAD
EDGE_COLS = Q_COLS + 2 * HEAD
FACTOR = HEAD ** (-0.5)
EXP_FACTOR = FACTOR * 1.4426950408889634
MASKED = -1e30
NT = (((1,), (1,)), ((), ()))
TN = (((0,), (0,)), ((), ()))

KEY_START = 0
LIVE = WIDE
OFFSET = 2 * WIDE
GROUP = OFFSET + 1
GROUPS = 8
PARTS = 4
PART = GROUP + GROUPS
RING_GROUPS = (0, 7, 1, 6, 2, 5, 3)
STEPS = (0, -1, 1, 2)


def rows_of(block, count=1):
    return pl.ds(block * BLOCK, count * BLOCK)


def dot(a, b, dims=None):
    if dims is None:
        return jnp.dot(a, b, preferred_element_type=jnp.float32)
    return lax.dot_general(a, b, dims, preferred_element_type=jnp.float32)


def fill_wide(wide, own, before, after, column):
    cols = slice(column, column + HEAD)
    wide[0:BLOCK] = before[:, cols]
    wide[BLOCK:BLOCK * (OWN + 1)] = own[...]
    wide[BLOCK * (OWN + 1):] = after[:, cols]


def query_block(own, before, after, block, head):
    cols = slice(head * HEAD, (head + 1) * HEAD)
    if block == 0:
        return before[:, cols]
    if block == WIDE - 1:
        return after[:, cols]
    return own[rows_of(block - 1), cols]


def context_place(block, chunk, outer_low, outer_high):
    if block == 0:
        return outer_low, rows_of(0)
    if block == WIDE - 1:
        return outer_high, rows_of(0)
    return chunk, rows_of({2: 0, 3: 1, 4: 2, 1: 3, 5: 4}[block])


def forward_kernel(table, q, k, v, before, after, chunk, outer_low, outer_high, k_wide, v_wide):
    fill_wide(k_wide, k, before, after, Q_COLS)
    v_wide[:, HEAD:] = jnp.ones((WIDE * BLOCK, HEAD), jnp.bfloat16)
    v_wide[0:BLOCK, :HEAD] = before[:, Q_COLS + HEAD:]
    v_wide[BLOCK:BLOCK * (OWN + 1), :HEAD] = v[...]
    v_wide[BLOCK * (OWN + 1):, :HEAD] = after[:, Q_COLS + HEAD:]
    for block in (2, 3, 4, 0, 1, 5, 6):
        target, rows = context_place(block, chunk, outer_low, outer_high)
        keys = (block + 1) * BLOCK

        def attend(block=block, target=target, rows=rows, keys=keys):
            row = lax.broadcasted_iota(jnp.int32, (BLOCK, keys), 0) + block * BLOCK
            col = lax.broadcasted_iota(jnp.int32, (BLOCK, keys), 1)
            allowed = (col <= row) & (col >= table[KEY_START + block] * BLOCK)
            bias = jnp.where(allowed, 0.0, MASKED)
            for head in range(HEADS):
                s = dot(query_block(q, before, after, block, head), k_wide[0:keys, :], NT)
                t = s * EXP_FACTOR + bias
                top = jnp.max(t, axis=1, keepdims=True)
                p = jnp.exp2(t - top).astype(jnp.bfloat16)
                both = dot(p, v_wide[0:keys, :])
                context = both[:, :HEAD] / both[:, HEAD:]
                target[rows, head * HEAD:(head + 1) * HEAD] = context.astype(jnp.bfloat16)

        if 2 <= block <= 4:
            attend()
        else:
            live = table[LIVE + block] != 0
            pl.when(live)(attend)

            @pl.when(jnp.logical_not(live))
            def _(target=target, rows=rows):
                target[rows, :] = jnp.zeros((BLOCK, Q_COLS), jnp.bfloat16)


def backward_kernel(
    blocks, earlier, table, q, k, v, before, after, grad, chunk, outer_low, outer_high, *refs
):
    last = len(earlier) == 2
    refs = list(refs)
    if earlier:
        sum_k_in, sum_v_in = refs[:2]
        parts = refs[2:2 + len(earlier)] if last else []
        refs = refs[2 + len(parts):]
    grad_q, out_k, out_v, k_wide, v_wide, k_turned, p_all, s_all = refs[:8]
    sum_k, sum_v = refs[8:] if last else (out_k, out_v)
    offset = table[OFFSET]
    fill_wide(k_wide, k, before, after, Q_COLS)
    fill_wide(v_wide, v, before, after, Q_COLS + HEAD)
    k_turned[...] = k_wide[...].T
    if earlier:
        sum_k[...] = sum_k_in[...]
        sum_v[...] = sum_v_in[...]
    else:
        sum_k[...] = jnp.zeros_like(sum_k)
        sum_v[...] = jnp.zeros_like(sum_v)
    if last:
        grad_q[...] = jnp.zeros_like(grad_q)

    def slot_of(block):
        return pl.ds(pl.multiple_of(jnp.clip(block - offset, 0, WIDE - 1) * BLOCK, BLOCK), BLOCK)

    def when_live(block, function):
        if 2 <= block <= 4:
            function()
        else:
            pl.when(table[LIVE + block] != 0)(function)

    for index, block in enumerate(blocks):

        def attend(index=index, block=block):
            source, rows = context_place(block, chunk, outer_low, outer_high)
            keys = (block + 1) * BLOCK
            slot = slot_of(block)
            target = slot if last else rows_of(index)
            col = lax.broadcasted_iota(jnp.int32, (keys, BLOCK), 1) + block * BLOCK
            row = lax.broadcasted_iota(jnp.int32, (keys, BLOCK), 0)
            allowed = (row <= col) & (row >= table[KEY_START + block] * BLOCK)
            bias = jnp.where(allowed, 0.0, MASKED)
            queries = []
            grads = []
            for head in range(HEADS):
                cols = slice(head * HEAD, (head + 1) * HEAD)
                qh = query_block(q, before, after, block, head)
                gh = grad[slot, cols]
                queries.append(qh)
                grads.append(gh)
                s = dot(k_wide[0:keys, :], qh, NT)
                t = s * EXP_FACTOR + bias
                top = jnp.max(t, axis=0, keepdims=True)
                w = jnp.exp2(t - top)
                p = w * (1.0 / jnp.sum(w, axis=0, keepdims=True))
                p_all[0:keys, cols] = p.astype(jnp.bfloat16)
                c = source[rows, cols].astype(jnp.float32)
                delta = jnp.sum((gh.astype(jnp.float32) * c).T, axis=0, keepdims=True)
                gp = dot(v_wide[0:keys, :], gh, NT)
                ds = (p * (gp - delta)).astype(jnp.bfloat16)
                s_all[0:keys, cols] = ds
                gq = dot(k_turned[:, 0:keys], ds)
                grad_q[target, cols] = (gq * FACTOR).T.astype(jnp.bfloat16)
            queries = jnp.concatenate(queries, axis=0)
            grads = jnp.concatenate(grads, axis=0)
            sum_v[0:keys, :] += dot(p_all[0:keys, :], grads)
            sum_k[0:keys, :] += dot(s_all[0:keys, :], queries)

        when_live(block, attend)
    if last:
        for part, made in zip(parts, earlier):
            for index, block in enumerate(made):

                def place(part=part, index=index, block=block):
                    grad_q[slot_of(block), :] = part[rows_of(index), :]

                when_live(block, place)
        shifted = pl.ds(pl.multiple_of(offset * BLOCK, BLOCK), WIDE * BLOCK)
        out_k[...] = (sum_k[shifted, :] * FACTOR).astype(jnp.bfloat16)
        out_v[...] = sum_v[shifted, :].astype(jnp.bfloat16)


ANY = pl.BlockSpec(memory_space=pl.ANY)
VMEM = pl.BlockSpec(memory_space=pltpu.VMEM)
SMEM = pl.BlockSpec(memory_space=pltpu.SMEM)


def half(rows, cols=Q_COLS):
    return jax.ShapeDtypeStruct((rows, cols), jnp.bfloat16)


def forward(table, q, k, v, before, after):
    return pl.pallas_call(
        forward_kernel,
        out_shape=(half(OWN * BLOCK), half(BLOCK), half(BLOCK)),
        in_specs=[SMEM] + [VMEM] * 5,
        out_specs=[VMEM] * 3,
        scratch_shapes=[
            pltpu.VMEM((WIDE * BLOCK, HEAD), jnp.bfloat16),
            pltpu.VMEM((WIDE * BLOCK, 2 * HEAD), jnp.bfloat16),
        ],
        compiler_params=pltpu.CompilerParams(vmem_limit_bytes=24 * 1024 * 1024),
        cost_estimate=pl.CostEstimate(flops=1_000_000, bytes_accessed=100_000, transcendentals=0),
        name="forward",
    )(table, q, k, v, before, after)


def backward(blocks, earlier, table, q, k, v, before, after, grad, contexts, sums=(), parts=()):
    last = len(earlier) == 2
    total = jax.ShapeDtypeStruct(((WIDE + 2) * BLOCK, HEAD), jnp.float32)
    operands = (q, k, v, before, after, grad, *contexts, *sums, *parts)
    return pl.pallas_call(
        functools.partial(backward_kernel, blocks, earlier),
        out_shape=(
            (half(WIDE * BLOCK), half(WIDE * BLOCK, HEAD), half(WIDE * BLOCK, HEAD))
            if last else (half(len(blocks) * BLOCK), total, total)
        ),
        in_specs=[SMEM] + [VMEM] * len(operands),
        out_specs=[VMEM] * 3,
        scratch_shapes=[
            pltpu.VMEM((WIDE * BLOCK, HEAD), jnp.bfloat16),
            pltpu.VMEM((WIDE * BLOCK, HEAD), jnp.bfloat16),
            pltpu.VMEM((HEAD, WIDE * BLOCK), jnp.bfloat16),
            pltpu.VMEM((WIDE * BLOCK, Q_COLS), jnp.bfloat16),
            pltpu.VMEM((WIDE * BLOCK, Q_COLS), jnp.bfloat16),
        ] + ([pltpu.VMEM(total.shape, total.dtype)] * 2 if last else []),
        compiler_params=pltpu.CompilerParams(vmem_limit_bytes=24 * 1024 * 1024),
        cost_estimate=pl.CostEstimate(flops=1_000_000, bytes_accessed=100_000, transcendentals=0),
        name="backward",
    )(table, *operands)


def merge_kernel(table, low_in, high_in, old, chunk):
    del old

    @pl.when(table[LIVE + 1] == 0)
    def _():
        chunk[rows_of(3), :] = low_in[...]

    @pl.when(table[LIVE + WIDE - 2] == 0)
    def _():
        chunk[rows_of(4), :] = high_in[...]


def merge(table, low_in, high_in, chunk):
    return pl.pallas_call(
        merge_kernel,
        out_shape=half(OWN * BLOCK),
        in_specs=[SMEM, VMEM, VMEM, VMEM],
        out_specs=VMEM,
        input_output_aliases={3: 0},
        compiler_params=pltpu.CompilerParams(vmem_limit_bytes=8 * 1024 * 1024),
        cost_estimate=pl.CostEstimate(flops=1_000_000, bytes_accessed=100_000, transcendentals=0),
        name="merge",
    )(table, low_in, high_in, chunk)


def gather_kernel(table, *refs):
    weights, chunks = refs[:GROUPS], refs[GROUPS:2 * GROUPS - 1]
    total, last_weight, held = refs[2 * GROUPS - 1:]
    for group, chunk in zip(RING_GROUPS, chunks):
        held[group] = chunk[...]

    def weight_block(index):
        return jnp.concatenate([weights[index][table[PART + part]] for part in range(PARTS)], axis=0)

    total[...] = jnp.zeros_like(total)
    for index in range(GROUPS):
        group = table[GROUP + index]

        @pl.when(group == GROUPS // 2)
        def _(index=index):
            last_weight[...] = weight_block(index)

        @pl.when(group != GROUPS // 2)
        def _(index=index, group=group):
            total[...] += dot(held[group], weight_block(index), NT)


def project_most(table, weights, chunks):
    return pl.pallas_call(
        gather_kernel,
        out_shape=(jax.ShapeDtypeStruct((OWN * BLOCK, Q_COLS), jnp.float32), half(Q_COLS)),
        in_specs=[SMEM] + [VMEM] * (len(weights) + len(chunks)),
        out_specs=[VMEM] * 2,
        scratch_shapes=[pltpu.VMEM((GROUPS, OWN * BLOCK, Q_COLS), jnp.bfloat16)],
        compiler_params=pltpu.CompilerParams(vmem_limit_bytes=32 * 1024 * 1024),
        cost_estimate=pl.CostEstimate(flops=1_000_000, bytes_accessed=100_000, transcendentals=0),
        name="project_most",
    )(table, *weights, *chunks)


def edge_kernel(weight, total, upper, lower, low, high):
    split = upper.shape[0]
    for block, target in ((3, low), (4, high)):
        rows = pl.ds(block * BLOCK - split, BLOCK)
        target[...] = (total[rows_of(block), :] + dot(lower[rows, :], weight[...], NT)).astype(jnp.bfloat16)


def project_edge(weight, total, upper, lower):
    return pl.pallas_call(
        edge_kernel,
        out_shape=(half(BLOCK), half(BLOCK)),
        in_specs=[VMEM] * 4,
        out_specs=[VMEM] * 2,
        compiler_params=pltpu.CompilerParams(vmem_limit_bytes=16 * 1024 * 1024),
        cost_estimate=pl.CostEstimate(flops=1_000_000, bytes_accessed=100_000, transcendentals=0),
        name="project_edge",
    )(weight, total, upper, lower)


def center_kernel(table, weight, total, first, second, low, high, projected):
    offset = table[OFFSET]
    split = first.shape[0]
    projected[...] = jnp.zeros_like(projected)

    def slot(block):
        return pl.ds(pl.multiple_of(jnp.clip(block - offset, 0, WIDE - 1) * BLOCK, BLOCK), BLOCK)

    upper = (total[0:split, :] + dot(first[...], weight[...], NT)).astype(jnp.bfloat16)
    rest = 3 * BLOCK - split
    lower = (total[split:3 * BLOCK, :] + dot(second[0:rest, :], weight[...], NT)).astype(jnp.bfloat16)
    start = pl.multiple_of(jnp.clip(2 - offset, 0, 2) * BLOCK, BLOCK)
    projected[pl.ds(start, split), :] = upper
    projected[pl.ds(pl.multiple_of(start + split, 64), rest), :] = lower
    for block, source in ((1, low), (WIDE - 2, high)):

        @pl.when(table[LIVE + block] != 0)
        def _(block=block, source=source):
            projected[slot(block), :] = source[...]


def project_center(table, weight, total, first, second, low, high):
    return pl.pallas_call(
        center_kernel,
        out_shape=half(WIDE * BLOCK),
        in_specs=[SMEM] + [VMEM] * 6,
        out_specs=VMEM,
        compiler_params=pltpu.CompilerParams(vmem_limit_bytes=16 * 1024 * 1024),
        cost_estimate=pl.CostEstimate(flops=1_000_000, bytes_accessed=100_000, transcendentals=0),
        name="project_center",
    )(table, weight, total, first, second, low, high)


def finish_kernel(table, outer_low, outer_high, old, projected, sems):
    del old
    offset = table[OFFSET]
    copies = []
    for index, (block, source) in enumerate(((0, outer_low), (WIDE - 1, outer_high))):
        start = pl.multiple_of(jnp.clip(block - offset, 0, WIDE - 1) * BLOCK, BLOCK)
        copy = pltpu.make_async_copy(source, projected.at[pl.ds(start, BLOCK), :], sems.at[index])
        copies.append((table[LIVE + block] != 0, copy))
    for live, copy in copies:
        pl.when(live)(copy.start)
    for live, copy in copies:
        pl.when(live)(copy.wait)


def finish(table, outer_low, outer_high, projected):
    return pl.pallas_call(
        finish_kernel,
        out_shape=half(WIDE * BLOCK),
        in_specs=[SMEM, VMEM, VMEM, ANY],
        out_specs=ANY,
        input_output_aliases={3: 0},
        scratch_shapes=[pltpu.SemaphoreType.DMA((2,))],
        compiler_params=pltpu.CompilerParams(vmem_limit_bytes=8 * 1024 * 1024),
        cost_estimate=pl.CostEstimate(flops=1_000_000, bytes_accessed=100_000, transcendentals=0),
        name="finish",
    )(table, outer_low, outer_high, projected)


def tables(doc_lengths, doc_owners, device):
    count = doc_lengths.shape[0]
    order = jnp.arange(count, dtype=jnp.int32)
    ends = jnp.sum(jnp.where(order[None, :] <= order[:, None], doc_lengths[None, :], 0), axis=1)
    first = jnp.sum(jnp.where(doc_owners < device, doc_lengths, 0))
    last = jnp.sum(jnp.where(doc_owners <= device, doc_lengths, 0))
    origin = device * OWN - 1
    block = origin + jnp.arange(WIDE, dtype=jnp.int32)
    start = jnp.max(jnp.where(ends[None, :] <= block[:, None], ends[None, :], 0), axis=1)
    start = jnp.clip(start - origin, 0, WIDE - 1)
    live = ((block >= first) & (block < last)).astype(jnp.int32)
    offset = jnp.clip(first - origin, 0, 2)
    x, y, core = device // 8, device // 2 % 4, device % 2
    groups = [(y + step) % 4 + 4 * (core ^ other) for other in range(2) for step in STEPS]
    parts = [sum(index * ((part - x - step) % 4 == 0) for index, step in enumerate(STEPS)) for part in range(PARTS)]
    places = jnp.stack([jnp.asarray(value, jnp.int32) for value in groups + parts])
    return jnp.concatenate([start, live, offset[None], places]).astype(jnp.int32)


def body(queries, key_states, window_values, doc_lengths, doc_owners, out_weight, grad_context):
    dp, tensor = lax.axis_size("dp"), lax.axis_size("tensor")
    device = lax.axis_index("dp")
    up = [(i, i + 1) for i in range(dp - 1)]
    down = [(i + 1, i) for i in range(dp - 1)]
    right = [(i, (i + 1) % tensor) for i in range(tensor)]
    left = [((i + 1) % tensor, i) for i in range(tensor)]
    table = tables(doc_lengths, doc_owners, device)

    def edge(rows):
        return jnp.concatenate([queries[rows], key_states[rows], window_values[rows]], axis=1)

    before = lax.ppermute(edge(slice((OWN - 1) * BLOCK, OWN * BLOCK)), "dp", up)
    after = lax.ppermute(edge(slice(0, BLOCK)), "dp", down)

    def tied(arrays, after):
        return lax.optimization_barrier((arrays, after))

    def shift(array, step):
        return lax.ppermute(array, "tensor", right if step > 0 else left)

    def fetch(array, axis, step):
        def source(i):
            place = [i // 8, i // 2 % 4, i % 2]
            place[axis] = (place[axis] + step) % (2 if axis == 2 else 4)
            return (place[0] * 4 + place[1]) * 2 + place[2]

        return lax.ppermute(array, "dp", [(source(i), i) for i in range(dp)])

    contexts = forward(table, queries, key_states, window_values, before, after)
    chunk, outer_low, outer_high = contexts

    turn = []
    for a in range(tensor):
        for b in range(tensor):
            g = (b - a) % tensor
            for e in range(PARTS):
                turn.append(((PARTS * a + e) * tensor + b, ((4 * e + g % 4) * 2 + g // 4) * tensor + a))
    piece = lax.ppermute(tied(out_weight.T, table)[0], ("dp", "tensor"), turn)

    low_in = lax.ppermute(outer_high, "dp", up)
    high_in = lax.ppermute(outer_low, "dp", down)
    chunk = merge(table, low_in, high_in, chunk)
    piece, chunk = tied(piece, chunk)
    contexts = (chunk, outer_low, outer_high)
    stages = ((1, 6), (2, 5), (0, 3, 4))

    def run_backward(stage, contexts, sums=(), parts=()):
        return backward(
            stages[stage], stages[:stage], table, queries, key_states, window_values, before, after, grad_context,
            contexts, sums, parts,
        )

    first_part, *sums = run_backward(0, contexts)
    row = [piece] + [fetch(piece, 0, step) for step in STEPS[1:]]
    row, (first_part, sums) = tied(row, (first_part, sums))
    going_right, going_left = shift(chunk, 1), shift(chunk, -1)
    (going_right, going_left), (first_part, sums) = tied((going_right, going_left), (first_part, sums))
    chunks = [chunk, going_right, going_left]
    plane = jnp.stack(row)
    second_part, *sums = run_backward(1, tied(contexts, (going_right, going_left, plane))[0], sums)
    weights = [plane] + [fetch(plane, 1, step) for step in STEPS[1:]]
    going_right, going_left = shift(going_right, 1), shift(going_left, -1)
    (going_right, going_left), (second_part, sums) = tied((going_right, going_left), (second_part, sums))
    chunks += [going_right, going_left]
    grads = run_backward(2, tied(contexts, (going_right, going_left))[0], sums, (first_part, second_part))
    going_right, going_left = shift(going_right, 1), shift(going_left, -1)
    weights, grads = tied(weights, grads)
    weights += [fetch(weight, 2, 1) for weight in weights]
    (going_right, going_left), grads = tied((going_right, going_left), grads)
    chunks += [going_right, going_left]
    rows = OWN * BLOCK // 2
    from_left = shift(going_right[rows:], 1)
    from_right = shift(going_left[:rows], -1)

    total, last_weight = project_most(table, weights, chunks)
    low_out, high_out = project_edge(last_weight, total, from_right, from_left)
    outer_low_out = lax.ppermute(high_out, "dp", up)
    outer_high_out = lax.ppermute(low_out, "dp", down)
    projected = project_center(table, last_weight, total, from_right, from_left, low_out, high_out)
    projected = finish(table, outer_low_out, outer_high_out, projected)
    return (projected, *grads)


def solution(mesh):
    placed = P("dp", "tensor")
    return jax.shard_map(
        body,
        mesh=mesh,
        in_specs=(placed, placed, placed, P(), P(), P("tensor", "dp"), placed),
        out_specs=(placed, placed, placed, placed),
        check_vma=False,
    )
```

```python
import functools

import jax
import jax.numpy as jnp
from jax import lax
from jax.experimental import pallas as pl
from jax.experimental.pallas import tpu as pltpu
from jax.sharding import PartitionSpec as P

HEAD = 128
BLOCK = 128
OWN = 5
WIDE = 7
HEADS = 5
Q_COLS = HEADS * HEAD
EDGE_COLS = Q_COLS + 2 * HEAD
FACTOR = HEAD ** (-0.5)
EXP_FACTOR = FACTOR * 1.4426950408889634
MASKED = -1e30
NT = (((1,), (1,)), ((), ()))
TN = (((0,), (0,)), ((), ()))

KEY_START = 0
LIVE = WIDE
OFFSET = 2 * WIDE
GROUP = OFFSET + 1
GROUPS = 8
PARTS = 4
PART = GROUP + GROUPS
SPAN_START = PART + PARTS
RING_GROUPS = (0, 7, 1, 6, 2, 5, 3)
LATER_GROUPS = (4,)
STEPS = (0, -1, 1, 2)
SPAN = 2 * OWN + 1


def rows_of(block, count=1):
    return pl.ds(block * BLOCK, count * BLOCK)


def dot(a, b, dims=None):
    if dims is None:
        return jnp.dot(a, b, preferred_element_type=jnp.float32)
    return lax.dot_general(a, b, dims, preferred_element_type=jnp.float32)


def fill_wide(wide, own, below, after, column):
    wide[0:BLOCK] = below[(OWN - 1) * BLOCK:, :]
    wide[BLOCK:BLOCK * (OWN + 1)] = own[...]
    wide[BLOCK * (OWN + 1):] = after[:, Q_COLS + column:Q_COLS + column + HEAD]


def query_block(own, before, after, block, head):
    cols = slice(head * HEAD, (head + 1) * HEAD)
    if block == 0:
        return before[:, cols]
    if block == WIDE - 1:
        return after[:, cols]
    return own[rows_of(block - 1), cols]


def forward_kernel(table, q, k, v, k_below, v_below, far_below, chunk, k_span, v_span):
    v_span[:, HEAD:] = jnp.ones((SPAN * BLOCK, HEAD), jnp.bfloat16)
    first, own = BLOCK, BLOCK * (OWN + 1)
    k_span[0:first] = far_below[:, :HEAD]
    k_span[first:own] = k_below[...]
    k_span[own:] = k[...]
    v_span[0:first, :HEAD] = far_below[:, HEAD:]
    v_span[first:own, :HEAD] = v_below[...]
    v_span[own:, :HEAD] = v[...]
    for block in range(OWN):
        begin, end = (0 if block == 0 else OWN) * BLOCK, (OWN + 2 + block) * BLOCK
        shape = (BLOCK, end - begin)
        row = lax.broadcasted_iota(jnp.int32, shape, 0) + (end - BLOCK)
        col = lax.broadcasted_iota(jnp.int32, shape, 1) + begin
        allowed = (col <= row) & (col >= table[SPAN_START + block] * BLOCK)
        bias = jnp.where(allowed, 0.0, MASKED)
        rows = rows_of((block - 1) if 1 <= block <= 3 else (3 if block == 0 else 4))
        for head in range(HEADS):
            cols = slice(head * HEAD, (head + 1) * HEAD)
            s = dot(q[rows_of(block), cols], k_span[begin:end, :], NT)
            t = s * EXP_FACTOR + bias
            top = jnp.max(t, axis=1, keepdims=True)
            p = jnp.exp2(t - top).astype(jnp.bfloat16)
            both = dot(p, v_span[begin:end, :])
            chunk[rows, cols] = (both[:, :HEAD] / both[:, HEAD:]).astype(jnp.bfloat16)


def backward_kernel(
    blocks, earlier, table, q, k, v, q_before, k_below, v_below, after, grad, *refs
):
    last = len(earlier) == 2
    refs = list(refs)
    if earlier:
        sum_k_in, sum_v_in = refs[:2]
        parts = refs[2:2 + len(earlier)] if last else []
        refs = refs[2 + len(parts):]
    grad_q, out_k, out_v, k_wide, v_wide, k_turned, p_all, s_all = refs[:8]
    sum_k, sum_v = refs[8:] if last else (out_k, out_v)
    offset = table[OFFSET]
    fill_wide(k_wide, k, k_below, after, 0)
    fill_wide(v_wide, v, v_below, after, HEAD)
    k_turned[...] = k_wide[...].T
    if earlier:
        sum_k[...] = sum_k_in[...]
        sum_v[...] = sum_v_in[...]
    else:
        sum_k[...] = jnp.zeros_like(sum_k)
        sum_v[...] = jnp.zeros_like(sum_v)
    if last:
        grad_q[...] = jnp.zeros_like(grad_q)

    def slot_of(block):
        return pl.ds(pl.multiple_of(jnp.clip(block - offset, 0, WIDE - 1) * BLOCK, BLOCK), BLOCK)

    def when_live(block, function):
        if 2 <= block <= 4:
            function()
        else:
            pl.when(table[LIVE + block] != 0)(function)

    for index, block in enumerate(blocks):

        def attend(index=index, block=block):
            keys = (block + 1) * BLOCK
            slot = slot_of(block)
            target = slot if last else rows_of(index)
            col = lax.broadcasted_iota(jnp.int32, (keys, BLOCK), 1) + block * BLOCK
            row = lax.broadcasted_iota(jnp.int32, (keys, BLOCK), 0)
            allowed = (row <= col) & (row >= table[KEY_START + block] * BLOCK)
            bias = jnp.where(allowed, 0.0, MASKED)
            queries = []
            grads = []
            for head in range(HEADS):
                cols = slice(head * HEAD, (head + 1) * HEAD)
                qh = query_block(q, q_before, after, block, head)
                gh = grad[slot, cols]
                queries.append(qh)
                grads.append(gh)
                s = dot(k_wide[0:keys, :], qh, NT)
                t = s * EXP_FACTOR + bias
                top = jnp.max(t, axis=0, keepdims=True)
                w = jnp.exp2(t - top)
                p = w * (1.0 / jnp.sum(w, axis=0, keepdims=True))
                p_all[0:keys, cols] = p.astype(jnp.bfloat16)
                gp = dot(v_wide[0:keys, :], gh, NT)
                delta = jnp.sum(p * gp, axis=0, keepdims=True)
                ds = (p * (gp - delta)).astype(jnp.bfloat16)
                s_all[0:keys, cols] = ds
                gq = dot(k_turned[:, 0:keys], ds)
                grad_q[target, cols] = (gq * FACTOR).T.astype(jnp.bfloat16)
            queries = jnp.concatenate(queries, axis=0)
            grads = jnp.concatenate(grads, axis=0)
            sum_v[0:keys, :] += dot(p_all[0:keys, :], grads)
            sum_k[0:keys, :] += dot(s_all[0:keys, :], queries)

        when_live(block, attend)
    if last:
        for part, made in zip(parts, earlier):
            for index, block in enumerate(made):

                def place(part=part, index=index, block=block):
                    grad_q[slot_of(block), :] = part[rows_of(index), :]

                when_live(block, place)
        shifted = pl.ds(pl.multiple_of(offset * BLOCK, BLOCK), WIDE * BLOCK)
        out_k[...] = (sum_k[shifted, :] * FACTOR).astype(jnp.bfloat16)
        out_v[...] = sum_v[shifted, :].astype(jnp.bfloat16)


ANY = pl.BlockSpec(memory_space=pl.ANY)
VMEM = pl.BlockSpec(memory_space=pltpu.VMEM)
SMEM = pl.BlockSpec(memory_space=pltpu.SMEM)


def half(rows, cols=Q_COLS):
    return jax.ShapeDtypeStruct((rows, cols), jnp.bfloat16)


def forward(table, q, k, v, k_below, v_below, far_below):
    return pl.pallas_call(
        forward_kernel,
        out_shape=half(OWN * BLOCK),
        in_specs=[SMEM] + [VMEM] * 6,
        out_specs=VMEM,
        scratch_shapes=[
            pltpu.VMEM((SPAN * BLOCK, HEAD), jnp.bfloat16),
            pltpu.VMEM((SPAN * BLOCK, 2 * HEAD), jnp.bfloat16),
        ],
        compiler_params=pltpu.CompilerParams(vmem_limit_bytes=24 * 1024 * 1024),
        cost_estimate=pl.CostEstimate(flops=1_000_000, bytes_accessed=100_000, transcendentals=0),
        name="forward",
    )(table, q, k, v, k_below, v_below, far_below)


def backward(blocks, earlier, table, operands, sums=(), parts=()):
    last = len(earlier) == 2
    total = jax.ShapeDtypeStruct(((WIDE + 2) * BLOCK, HEAD), jnp.float32)
    operands = (*operands, *sums, *parts)
    return pl.pallas_call(
        functools.partial(backward_kernel, blocks, earlier),
        out_shape=(
            (half(WIDE * BLOCK), half(WIDE * BLOCK, HEAD), half(WIDE * BLOCK, HEAD))
            if last else (half(len(blocks) * BLOCK), total, total)
        ),
        in_specs=[SMEM] + [VMEM] * len(operands),
        out_specs=[VMEM] * 3,
        scratch_shapes=[
            pltpu.VMEM((WIDE * BLOCK, HEAD), jnp.bfloat16),
            pltpu.VMEM((WIDE * BLOCK, HEAD), jnp.bfloat16),
            pltpu.VMEM((HEAD, WIDE * BLOCK), jnp.bfloat16),
            pltpu.VMEM((WIDE * BLOCK, Q_COLS), jnp.bfloat16),
            pltpu.VMEM((WIDE * BLOCK, Q_COLS), jnp.bfloat16),
        ] + ([pltpu.VMEM(total.shape, total.dtype)] * 2 if last else []),
        compiler_params=pltpu.CompilerParams(vmem_limit_bytes=24 * 1024 * 1024),
        cost_estimate=pl.CostEstimate(flops=1_000_000, bytes_accessed=100_000, transcendentals=0),
        name="backward",
    )(table, *operands)


def most_kernel(groups, table, *refs):
    weights, chunks = refs[:GROUPS], refs[GROUPS:GROUPS + len(groups)]
    total, *last, held = refs[GROUPS + len(groups):]
    for index, weight in enumerate(weights):
        held[table[GROUP + index]] = jnp.concatenate([weight[table[PART + part]] for part in range(PARTS)], axis=0)
    for group, target in zip(LATER_GROUPS, last):
        target[...] = held[group]
    for place, (group, chunk) in enumerate(zip(groups, chunks)):
        both = dot(chunk[...], held[group], NT)
        if place == 0:
            total[...] = both
        else:
            total[...] += both


def project_most(table, weights, chunks):
    groups = RING_GROUPS[:len(chunks)]
    return pl.pallas_call(
        functools.partial(most_kernel, groups),
        out_shape=(jax.ShapeDtypeStruct((OWN * BLOCK, Q_COLS), jnp.float32),) + (half(Q_COLS),) * len(LATER_GROUPS),
        in_specs=[SMEM] + [VMEM] * (len(weights) + len(chunks)),
        out_specs=[VMEM] * (1 + len(LATER_GROUPS)),
        scratch_shapes=[pltpu.VMEM((GROUPS, Q_COLS, Q_COLS), jnp.bfloat16)],
        compiler_params=pltpu.CompilerParams(vmem_limit_bytes=32 * 1024 * 1024),
        cost_estimate=pl.CostEstimate(flops=1_000_000, bytes_accessed=100_000, transcendentals=0),
        name="project_most",
    )(table, *weights, *chunks)


def edge_kernel(weight, total, edges, low, high):
    for block, target in ((3, low), (4, high)):
        product = dot(edges[rows_of(block - 3), :], weight[...], NT)
        target[...] = (total[rows_of(block), :] + product).astype(jnp.bfloat16)


def project_edge(weight, total, edges):
    return pl.pallas_call(
        edge_kernel,
        out_shape=(half(BLOCK), half(BLOCK)),
        in_specs=[VMEM] * 3,
        out_specs=[VMEM] * 2,
        compiler_params=pltpu.CompilerParams(vmem_limit_bytes=16 * 1024 * 1024),
        cost_estimate=pl.CostEstimate(flops=1_000_000, bytes_accessed=100_000, transcendentals=0),
        name="project_edge",
    )(weight, total, edges)


def center_kernel(table, weight, total, center, low, high, projected):
    offset = table[OFFSET]
    projected[...] = jnp.zeros_like(projected)

    def slot(block):
        return pl.ds(pl.multiple_of(jnp.clip(block - offset, 0, WIDE - 1) * BLOCK, BLOCK), BLOCK)

    start = pl.multiple_of(jnp.clip(2 - offset, 0, 2) * BLOCK, BLOCK)
    product = dot(center[...], weight[...], NT)
    projected[pl.ds(start, 3 * BLOCK), :] = (total[rows_of(0, 3), :] + product).astype(jnp.bfloat16)
    for block, source in ((1, low), (WIDE - 2, high)):

        @pl.when(table[LIVE + block] != 0)
        def _(block=block, source=source):
            projected[slot(block), :] = source[...]


def project_center(table, weight, total, center, low, high):
    return pl.pallas_call(
        center_kernel,
        out_shape=half(WIDE * BLOCK),
        in_specs=[SMEM] + [VMEM] * 5,
        out_specs=VMEM,
        compiler_params=pltpu.CompilerParams(vmem_limit_bytes=16 * 1024 * 1024),
        cost_estimate=pl.CostEstimate(flops=1_000_000, bytes_accessed=100_000, transcendentals=0),
        name="project_center",
    )(table, weight, total, center, low, high)


def finish_kernel(table, outer_low, outer_high, old, projected, sems):
    del old
    offset = table[OFFSET]
    copies = []
    for index, (block, source) in enumerate(((0, outer_low), (WIDE - 1, outer_high))):
        start = pl.multiple_of(jnp.clip(block - offset, 0, WIDE - 1) * BLOCK, BLOCK)
        copy = pltpu.make_async_copy(source, projected.at[pl.ds(start, BLOCK), :], sems.at[index])
        copies.append((table[LIVE + block] != 0, copy))
    for live, copy in copies:
        pl.when(live)(copy.start)
    for live, copy in copies:
        pl.when(live)(copy.wait)


def finish(table, outer_low, outer_high, projected):
    return pl.pallas_call(
        finish_kernel,
        out_shape=half(WIDE * BLOCK),
        in_specs=[SMEM, VMEM, VMEM, ANY],
        out_specs=ANY,
        input_output_aliases={3: 0},
        scratch_shapes=[pltpu.SemaphoreType.DMA((2,))],
        compiler_params=pltpu.CompilerParams(vmem_limit_bytes=8 * 1024 * 1024),
        cost_estimate=pl.CostEstimate(flops=1_000_000, bytes_accessed=100_000, transcendentals=0),
        name="finish",
    )(table, outer_low, outer_high, projected)


def tables(doc_lengths, doc_owners, device):
    count = doc_lengths.shape[0]
    order = jnp.arange(count, dtype=jnp.int32)
    ends = jnp.sum(jnp.where(order[None, :] <= order[:, None], doc_lengths[None, :], 0), axis=1)
    first = jnp.sum(jnp.where(doc_owners < device, doc_lengths, 0))
    last = jnp.sum(jnp.where(doc_owners <= device, doc_lengths, 0))
    origin = device * OWN - 1
    block = origin + jnp.arange(WIDE, dtype=jnp.int32)
    start = jnp.max(jnp.where(ends[None, :] <= block[:, None], ends[None, :], 0), axis=1)
    span_start = jnp.clip(start[1:1 + OWN] - (origin - OWN), 0, SPAN - 1)
    start = jnp.clip(start - origin, 0, WIDE - 1)
    live = ((block >= first) & (block < last)).astype(jnp.int32)
    offset = jnp.clip(first - origin, 0, 2)
    x, y, core = device // 8, device // 2 % 4, device % 2
    groups = [(y + step) % 4 + 4 * (core ^ other) for other in range(2) for step in STEPS]
    parts = [sum(index * ((part - x - step) % 4 == 0) for index, step in enumerate(STEPS)) for part in range(PARTS)]
    places = jnp.stack([jnp.asarray(value, jnp.int32) for value in groups + parts])
    return jnp.concatenate([start, live, offset[None], places, span_start]).astype(jnp.int32)


def body(queries, key_states, window_values, doc_lengths, doc_owners, out_weight, grad_context):
    dp, tensor = lax.axis_size("dp"), lax.axis_size("tensor")
    device = lax.axis_index("dp")
    up = [(i, i + 1) for i in range(dp - 1)]
    down = [(i + 1, i) for i in range(dp - 1)]
    right = [(i, (i + 1) % tensor) for i in range(tensor)]
    left = [((i + 1) % tensor, i) for i in range(tensor)]
    table = tables(doc_lengths, doc_owners, device)

    def tied(arrays, after):
        return lax.optimization_barrier((arrays, after))

    def shift(array, step):
        return lax.ppermute(array, "tensor", right if step > 0 else left)

    def fetch(array, axis, step):
        def source(i):
            place = [i // 8, i // 2 % 4, i % 2]
            place[axis] = (place[axis] + step) % (2 if axis == 2 else 4)
            return (place[0] * 4 + place[1]) * 2 + place[2]

        return lax.ppermute(array, "dp", [(source(i), i) for i in range(dp)])

    turn = []
    for a in range(tensor):
        for b in range(tensor):
            g = (b - a) % tensor
            for e in range(PARTS):
                turn.append(((PARTS * a + e) * tensor + b, ((4 * e + g % 4) * 2 + g // 4) * tensor + a))
    piece = lax.ppermute(out_weight.T, ("dp", "tensor"), turn)

    last = slice((OWN - 1) * BLOCK, OWN * BLOCK)
    (own_keys, own_values), table = tied((key_states, window_values), table)
    below = (lax.ppermute(own_keys, "dp", up), lax.ppermute(own_values, "dp", up))
    far_below = lax.ppermute(
        jnp.concatenate([own_keys[last], own_values[last]], axis=1), "dp", [(i, i + 2) for i in range(dp - 2)]
    )

    piece, (below, far_below) = tied(piece, (below, far_below))
    chunk = forward(table, queries, key_states, window_values, *below, far_below)

    (edge_queries, edge_keys, edge_values), _ = tied((queries, key_states, window_values), chunk)
    q_before = lax.ppermute(edge_queries[last], "dp", up)
    after = lax.ppermute(
        jnp.concatenate([edge_queries[:BLOCK], edge_keys[:BLOCK], edge_values[:BLOCK]], axis=1), "dp", down
    )
    operands = (queries, key_states, window_values, q_before, *below, after, grad_context)
    stages = ((1, 6), (2, 5), (0, 3, 4))

    def run_backward(stage, operands, sums=(), parts=()):
        return backward(stages[stage], stages[:stage], table, operands, sums, parts)

    pieces = [piece] + [fetch(piece, 0, step) for step in STEPS[1:]]
    first_part, *sums = run_backward(0, operands)
    going_right, going_left = shift(chunk, 1), shift(chunk, -1)
    (going_right, going_left, pieces), (first_part, sums) = tied(
        (going_right, going_left, pieces), (first_part, sums)
    )
    chunks = [chunk, going_right, going_left]
    near = jnp.stack(pieces)
    second_part, *sums = run_backward(1, tied(operands, (going_right, going_left, near))[0], sums)
    sides = [fetch(near, 1, step) for step in STEPS[1:]]
    going_right, going_left = shift(going_right, 1), shift(going_left, -1)
    (going_right, going_left), (second_part, sums) = tied((going_right, going_left), (second_part, sums))
    chunks += [going_right, going_left]
    grads = run_backward(2, tied(operands, (going_right, going_left))[0], sums, (first_part, second_part))
    going_right, going_left = shift(going_right, 1), shift(going_left, -1)
    sides, grads = tied(sides, grads)
    weights = [near] + sides
    weights += [fetch(weight, 2, 1) for weight in weights]
    (going_right, going_left), grads = tied((going_right, going_left), grads)
    chunks += [going_right, going_left]
    edges = shift(going_right[3 * BLOCK:], 1)
    center = shift(going_left[:3 * BLOCK], -1)
    total, last_weight = project_most(table, weights, chunks)
    low_out, high_out = project_edge(last_weight, total, edges)
    outer_low_out = lax.ppermute(high_out, "dp", up)
    outer_high_out = lax.ppermute(low_out, "dp", down)
    projected = project_center(table, last_weight, total, center, low_out, high_out)
    projected = finish(table, outer_low_out, outer_high_out, projected)
    return (projected, *grads)


def solution(mesh):
    placed = P("dp", "tensor")
    return jax.shard_map(
        body,
        mesh=mesh,
        in_specs=(placed, placed, placed, P(), P(), P("tensor", "dp"), placed),
        out_specs=(placed, placed, placed, placed),
        check_vma=False,
    )
```

```python
import functools

import jax
import jax.numpy as jnp
from jax import lax
from jax.experimental import pallas as pl
from jax.experimental.pallas import tpu as pltpu
from jax.sharding import PartitionSpec as P

HEAD = 128
BLOCK = 128
OWN = 5
WIDE = 7
HEADS = 5
Q_COLS = HEADS * HEAD
EDGE_COLS = Q_COLS + 2 * HEAD
FACTOR = HEAD ** (-0.5)
EXP_FACTOR = FACTOR * 1.4426950408889634
MASKED = -1e30
NT = (((1,), (1,)), ((), ()))
TN = (((0,), (0,)), ((), ()))

KEY_START = 0
LIVE = WIDE
OFFSET = 2 * WIDE
GROUP = OFFSET + 1
GROUPS = 8
PARTS = 4
PART = GROUP + GROUPS
SPAN_START = PART + PARTS
RING_GROUPS = (0, 7, 1, 6, 2, 5, 3)
LATER_GROUPS = (4,)
STEPS = (0, -1, 1, 2)
SPAN = 2 * OWN + 1


def rows_of(block, count=1):
    return pl.ds(block * BLOCK, count * BLOCK)


def dot(a, b, dims=None):
    if dims is None:
        return jnp.dot(a, b, preferred_element_type=jnp.float32)
    return lax.dot_general(a, b, dims, preferred_element_type=jnp.float32)


def fill_wide(wide, own, below, after, column):
    wide[0:BLOCK] = below[(OWN - 1) * BLOCK:, :]
    wide[BLOCK:BLOCK * (OWN + 1)] = own[...]
    wide[BLOCK * (OWN + 1):] = after[:, Q_COLS + column:Q_COLS + column + HEAD]


def query_block(own, before, after, block, head):
    cols = slice(head * HEAD, (head + 1) * HEAD)
    if block == 0:
        return before[:, cols]
    if block == WIDE - 1:
        return after[:, cols]
    return own[rows_of(block - 1), cols]


def forward_kernel(table, q, k, v, k_below, v_below, far_below, chunk, k_span, v_span):
    v_span[:, HEAD:] = jnp.ones((SPAN * BLOCK, HEAD), jnp.bfloat16)
    first, own = BLOCK, BLOCK * (OWN + 1)
    k_span[0:first] = far_below[:, :HEAD]
    k_span[first:own] = k_below[...]
    k_span[own:] = k[...]
    v_span[0:first, :HEAD] = far_below[:, HEAD:]
    v_span[first:own, :HEAD] = v_below[...]
    v_span[own:, :HEAD] = v[...]
    for block in range(OWN):
        begin, end = (0 if block == 0 else OWN) * BLOCK, (OWN + 2 + block) * BLOCK
        shape = (BLOCK, end - begin)
        row = lax.broadcasted_iota(jnp.int32, shape, 0) + (end - BLOCK)
        col = lax.broadcasted_iota(jnp.int32, shape, 1) + begin
        allowed = (col <= row) & (col >= table[SPAN_START + block] * BLOCK)
        bias = jnp.where(allowed, 0.0, MASKED)
        rows = rows_of((block - 1) if 1 <= block <= 3 else (3 if block == 0 else 4))
        for head in range(HEADS):
            cols = slice(head * HEAD, (head + 1) * HEAD)
            s = dot(q[rows_of(block), cols], k_span[begin:end, :], NT)
            t = s * EXP_FACTOR + bias
            top = jnp.max(t, axis=1, keepdims=True)
            p = jnp.exp2(t - top).astype(jnp.bfloat16)
            both = dot(p, v_span[begin:end, :])
            chunk[rows, cols] = (both[:, :HEAD] / both[:, HEAD:]).astype(jnp.bfloat16)


def backward_kernel(
    blocks, earlier, table, q, k, v, q_before, k_below, v_below, after, grad, *refs
):
    last = len(earlier) == 2
    refs = list(refs)
    if earlier:
        sum_k_in, sum_v_in = refs[:2]
        parts = refs[2:2 + len(earlier)] if last else []
        refs = refs[2 + len(parts):]
    grad_q, out_k, out_v, k_wide, v_wide, k_turned, p_all, s_all = refs[:8]
    sum_k, sum_v = refs[8:] if last else (out_k, out_v)
    offset = table[OFFSET]
    fill_wide(k_wide, k, k_below, after, 0)
    fill_wide(v_wide, v, v_below, after, HEAD)
    k_turned[...] = k_wide[...].T
    if earlier:
        sum_k[...] = sum_k_in[...]
        sum_v[...] = sum_v_in[...]
    else:
        sum_k[...] = jnp.zeros_like(sum_k)
        sum_v[...] = jnp.zeros_like(sum_v)
    if last:
        grad_q[...] = jnp.zeros_like(grad_q)

    def slot_of(block):
        return pl.ds(pl.multiple_of(jnp.clip(block - offset, 0, WIDE - 1) * BLOCK, BLOCK), BLOCK)

    def when_live(block, function):
        if 2 <= block <= 4:
            function()
        else:
            pl.when(table[LIVE + block] != 0)(function)

    for index, block in enumerate(blocks):

        def attend(index=index, block=block):
            keys = (block + 1) * BLOCK
            slot = slot_of(block)
            target = slot if last else rows_of(index)
            col = lax.broadcasted_iota(jnp.int32, (keys, BLOCK), 1) + block * BLOCK
            row = lax.broadcasted_iota(jnp.int32, (keys, BLOCK), 0)
            allowed = (row <= col) & (row >= table[KEY_START + block] * BLOCK)
            bias = jnp.where(allowed, 0.0, MASKED)
            queries = []
            grads = []
            for head in range(HEADS):
                cols = slice(head * HEAD, (head + 1) * HEAD)
                qh = query_block(q, q_before, after, block, head)
                gh = grad[slot, cols]
                queries.append(qh)
                grads.append(gh)
                s = dot(k_wide[0:keys, :], qh, NT)
                t = s * EXP_FACTOR + bias
                top = jnp.max(t, axis=0, keepdims=True)
                w = jnp.exp2(t - top)
                p = w * (1.0 / jnp.sum(w, axis=0, keepdims=True))
                p_all[0:keys, cols] = p.astype(jnp.bfloat16)
                gp = dot(v_wide[0:keys, :], gh, NT)
                delta = jnp.sum(p * gp, axis=0, keepdims=True)
                ds = (p * (gp - delta)).astype(jnp.bfloat16)
                s_all[0:keys, cols] = ds
                gq = dot(k_turned[:, 0:keys], ds)
                grad_q[target, cols] = (gq * FACTOR).T.astype(jnp.bfloat16)
            queries = jnp.concatenate(queries, axis=0)
            grads = jnp.concatenate(grads, axis=0)
            sum_v[0:keys, :] += dot(p_all[0:keys, :], grads)
            sum_k[0:keys, :] += dot(s_all[0:keys, :], queries)

        when_live(block, attend)
    if last:
        for part, made in zip(parts, earlier):
            for index, block in enumerate(made):

                def place(part=part, index=index, block=block):
                    grad_q[slot_of(block), :] = part[rows_of(index), :]

                when_live(block, place)
        shifted = pl.ds(pl.multiple_of(offset * BLOCK, BLOCK), WIDE * BLOCK)
        out_k[...] = (sum_k[shifted, :] * FACTOR).astype(jnp.bfloat16)
        out_v[...] = sum_v[shifted, :].astype(jnp.bfloat16)


ANY = pl.BlockSpec(memory_space=pl.ANY)
VMEM = pl.BlockSpec(memory_space=pltpu.VMEM)
SMEM = pl.BlockSpec(memory_space=pltpu.SMEM)


def half(rows, cols=Q_COLS):
    return jax.ShapeDtypeStruct((rows, cols), jnp.bfloat16)


def forward(table, q, k, v, k_below, v_below, far_below):
    return pl.pallas_call(
        forward_kernel,
        out_shape=half(OWN * BLOCK),
        in_specs=[SMEM] + [VMEM] * 6,
        out_specs=VMEM,
        scratch_shapes=[
            pltpu.VMEM((SPAN * BLOCK, HEAD), jnp.bfloat16),
            pltpu.VMEM((SPAN * BLOCK, 2 * HEAD), jnp.bfloat16),
        ],
        compiler_params=pltpu.CompilerParams(vmem_limit_bytes=58 * 1024 * 1024),
        cost_estimate=pl.CostEstimate(flops=1_000_000, bytes_accessed=100_000, transcendentals=0),
        name="forward",
    )(table, q, k, v, k_below, v_below, far_below)


def backward(blocks, earlier, table, operands, sums=(), parts=()):
    last = len(earlier) == 2
    total = jax.ShapeDtypeStruct(((WIDE + 2) * BLOCK, HEAD), jnp.float32)
    operands = (*operands, *sums, *parts)
    return pl.pallas_call(
        functools.partial(backward_kernel, blocks, earlier),
        out_shape=(
            (half(WIDE * BLOCK), half(WIDE * BLOCK, HEAD), half(WIDE * BLOCK, HEAD))
            if last else (half(len(blocks) * BLOCK), total, total)
        ),
        in_specs=[SMEM] + [VMEM] * len(operands),
        out_specs=[VMEM] * 3,
        scratch_shapes=[
            pltpu.VMEM((WIDE * BLOCK, HEAD), jnp.bfloat16),
            pltpu.VMEM((WIDE * BLOCK, HEAD), jnp.bfloat16),
            pltpu.VMEM((HEAD, WIDE * BLOCK), jnp.bfloat16),
            pltpu.VMEM((WIDE * BLOCK, Q_COLS), jnp.bfloat16),
            pltpu.VMEM((WIDE * BLOCK, Q_COLS), jnp.bfloat16),
        ] + ([pltpu.VMEM(total.shape, total.dtype)] * 2 if last else []),
        compiler_params=pltpu.CompilerParams(vmem_limit_bytes=24 * 1024 * 1024),
        cost_estimate=pl.CostEstimate(flops=1_000_000, bytes_accessed=100_000, transcendentals=0),
        name="backward",
    )(table, *operands)


def most_kernel(groups, table, *refs):
    weights, chunks = refs[:GROUPS], refs[GROUPS:GROUPS + len(groups)]
    total, *last, held = refs[GROUPS + len(groups):]
    for index, weight in enumerate(weights):
        held[table[GROUP + index]] = jnp.concatenate([weight[table[PART + part]] for part in range(PARTS)], axis=0)
    for group, target in zip(LATER_GROUPS, last):
        target[...] = held[group]
    for place, (group, chunk) in enumerate(zip(groups, chunks)):
        both = dot(chunk[...], held[group], NT)
        if place == 0:
            total[...] = both
        else:
            total[...] += both


def project_most(table, weights, chunks):
    groups = RING_GROUPS[:len(chunks)]
    return pl.pallas_call(
        functools.partial(most_kernel, groups),
        out_shape=(jax.ShapeDtypeStruct((OWN * BLOCK, Q_COLS), jnp.float32),) + (half(Q_COLS),) * len(LATER_GROUPS),
        in_specs=[SMEM] + [VMEM] * (len(weights) + len(chunks)),
        out_specs=[VMEM] * (1 + len(LATER_GROUPS)),
        scratch_shapes=[pltpu.VMEM((GROUPS, Q_COLS, Q_COLS), jnp.bfloat16)],
        compiler_params=pltpu.CompilerParams(vmem_limit_bytes=32 * 1024 * 1024),
        cost_estimate=pl.CostEstimate(flops=1_000_000, bytes_accessed=100_000, transcendentals=0),
        name="project_most",
    )(table, *weights, *chunks)


def edge_kernel(weight, total, edges, low, high):
    for block, target in ((3, low), (4, high)):
        product = dot(edges[rows_of(block - 3), :], weight[...], NT)
        target[...] = (total[rows_of(block), :] + product).astype(jnp.bfloat16)


def project_edge(weight, total, edges):
    return pl.pallas_call(
        edge_kernel,
        out_shape=(half(BLOCK), half(BLOCK)),
        in_specs=[VMEM] * 3,
        out_specs=[VMEM] * 2,
        compiler_params=pltpu.CompilerParams(vmem_limit_bytes=16 * 1024 * 1024),
        cost_estimate=pl.CostEstimate(flops=1_000_000, bytes_accessed=100_000, transcendentals=0),
        name="project_edge",
    )(weight, total, edges)


def center_kernel(table, weight, total, center, low, high, projected):
    offset = table[OFFSET]
    projected[...] = jnp.zeros_like(projected)

    def slot(block):
        return pl.ds(pl.multiple_of(jnp.clip(block - offset, 0, WIDE - 1) * BLOCK, BLOCK), BLOCK)

    start = pl.multiple_of(jnp.clip(2 - offset, 0, 2) * BLOCK, BLOCK)
    product = dot(center[...], weight[...], NT)
    projected[pl.ds(start, 3 * BLOCK), :] = (total[rows_of(0, 3), :] + product).astype(jnp.bfloat16)
    for block, source in ((1, low), (WIDE - 2, high)):

        @pl.when(table[LIVE + block] != 0)
        def _(block=block, source=source):
            projected[slot(block), :] = source[...]


def project_center(table, weight, total, center, low, high):
    return pl.pallas_call(
        center_kernel,
        out_shape=half(WIDE * BLOCK),
        in_specs=[SMEM] + [VMEM] * 5,
        out_specs=VMEM,
        compiler_params=pltpu.CompilerParams(vmem_limit_bytes=16 * 1024 * 1024),
        cost_estimate=pl.CostEstimate(flops=1_000_000, bytes_accessed=100_000, transcendentals=0),
        name="project_center",
    )(table, weight, total, center, low, high)


def finish_kernel(table, outer_low, outer_high, old, projected, sems):
    del old
    offset = table[OFFSET]
    copies = []
    for index, (block, source) in enumerate(((0, outer_low), (WIDE - 1, outer_high))):
        start = pl.multiple_of(jnp.clip(block - offset, 0, WIDE - 1) * BLOCK, BLOCK)
        copy = pltpu.make_async_copy(source, projected.at[pl.ds(start, BLOCK), :], sems.at[index])
        copies.append((table[LIVE + block] != 0, copy))
    for live, copy in copies:
        pl.when(live)(copy.start)
    for live, copy in copies:
        pl.when(live)(copy.wait)


def finish(table, outer_low, outer_high, projected):
    return pl.pallas_call(
        finish_kernel,
        out_shape=half(WIDE * BLOCK),
        in_specs=[SMEM, VMEM, VMEM, ANY],
        out_specs=ANY,
        input_output_aliases={3: 0},
        scratch_shapes=[pltpu.SemaphoreType.DMA((2,))],
        compiler_params=pltpu.CompilerParams(vmem_limit_bytes=8 * 1024 * 1024),
        cost_estimate=pl.CostEstimate(flops=1_000_000, bytes_accessed=100_000, transcendentals=0),
        name="finish",
    )(table, outer_low, outer_high, projected)


def tables(doc_lengths, doc_owners, device):
    count = doc_lengths.shape[0]
    order = jnp.arange(count, dtype=jnp.int32)
    ends = jnp.sum(jnp.where(order[None, :] <= order[:, None], doc_lengths[None, :], 0), axis=1)
    origin = device * OWN - 1
    block = origin + jnp.arange(WIDE, dtype=jnp.int32)
    limit = jnp.concatenate([block, device[None] - 1, device[None]]).astype(jnp.int32)
    by_owner = jnp.arange(WIDE + 2) >= WIDE
    key = jnp.where(by_owner[:, None], doc_owners[None, :], ends[None, :])
    marks = jnp.max(jnp.where(key <= limit[:, None], ends[None, :], 0), axis=1)
    start, first, last = marks[:WIDE], marks[WIDE], marks[WIDE + 1]
    span_start = jnp.clip(start[1:1 + OWN] - (origin - OWN), 0, SPAN - 1)
    start = jnp.clip(start - origin, 0, WIDE - 1)
    live = ((block >= first) & (block < last)).astype(jnp.int32)
    offset = jnp.clip(first - origin, 0, 2)
    x, y, core = device // 8, device // 2 % 4, device % 2
    groups = [(y + step) % 4 + 4 * (core ^ other) for other in range(2) for step in STEPS]
    parts = [sum(index * ((part - x - step) % 4 == 0) for index, step in enumerate(STEPS)) for part in range(PARTS)]
    places = jnp.stack([jnp.asarray(value, jnp.int32) for value in groups + parts])
    return jnp.concatenate([start, live, offset[None], places, span_start]).astype(jnp.int32)


def body(queries, key_states, window_values, doc_lengths, doc_owners, out_weight, grad_context):
    dp, tensor = lax.axis_size("dp"), lax.axis_size("tensor")
    device = lax.axis_index("dp")
    up = [(i, i + 1) for i in range(dp - 1)]
    down = [(i + 1, i) for i in range(dp - 1)]
    right = [(i, (i + 1) % tensor) for i in range(tensor)]
    left = [((i + 1) % tensor, i) for i in range(tensor)]
    table = tables(doc_lengths, doc_owners, device)

    def tied(arrays, after):
        return lax.optimization_barrier((arrays, after))

    def shift(array, step):
        return lax.ppermute(array, "tensor", right if step > 0 else left)

    def fetch(array, axis, step):
        def source(i):
            place = [i // 8, i // 2 % 4, i % 2]
            place[axis] = (place[axis] + step) % (2 if axis == 2 else 4)
            return (place[0] * 4 + place[1]) * 2 + place[2]

        return lax.ppermute(array, "dp", [(source(i), i) for i in range(dp)])

    turn = []
    for a in range(tensor):
        for b in range(tensor):
            g = (b - a) % tensor
            for e in range(PARTS):
                turn.append(((PARTS * a + e) * tensor + b, ((4 * e + g % 4) * 2 + g // 4) * tensor + a))
    piece = lax.ppermute(out_weight.T, ("dp", "tensor"), turn)

    last = slice((OWN - 1) * BLOCK, OWN * BLOCK)
    (own_keys, own_values), table = tied((key_states, window_values), table)
    below = (lax.ppermute(own_keys, "dp", up), lax.ppermute(own_values, "dp", up))
    far_below = lax.ppermute(
        jnp.concatenate([own_keys[last], own_values[last]], axis=1), "dp", [(i, i + 2) for i in range(dp - 2)]
    )

    piece, (below, far_below) = tied(piece, (below, far_below))
    chunk = forward(table, queries, key_states, window_values, *below, far_below)

    (edge_queries, edge_keys, edge_values), _ = tied((queries, key_states, window_values), chunk)
    q_before = lax.ppermute(edge_queries[last], "dp", up)
    after = lax.ppermute(
        jnp.concatenate([edge_queries[:BLOCK], edge_keys[:BLOCK], edge_values[:BLOCK]], axis=1), "dp", down
    )
    operands = (queries, key_states, window_values, q_before, *below, after, grad_context)
    stages = ((0, 1), (2, 3, 6), (4, 5))

    def run_backward(stage, operands, sums=(), parts=()):
        return backward(stages[stage], stages[:stage], table, operands, sums, parts)

    pieces = [piece] + [fetch(piece, 0, step) for step in STEPS[1:]]
    first_part, *sums = run_backward(0, operands)
    going_right, going_left = shift(chunk, 1), shift(chunk, -1)
    (going_right, going_left, pieces), (first_part, sums) = tied(
        (going_right, going_left, pieces), (first_part, sums)
    )
    chunks = [chunk, going_right, going_left]
    near = jnp.stack(pieces)
    second_part, *sums = run_backward(1, tied(operands, (going_right, going_left, near))[0], sums)
    sides = [fetch(near, 1, step) for step in STEPS[1:]]
    going_right, going_left = shift(going_right, 1), shift(going_left, -1)
    (going_right, going_left), (second_part, sums) = tied((going_right, going_left), (second_part, sums))
    chunks += [going_right, going_left]
    grads = run_backward(2, tied(operands, (going_right, going_left))[0], sums, (first_part, second_part))
    going_right, going_left = shift(going_right, 1), shift(going_left, -1)
    sides, grads = tied(sides, grads)
    weights = [near] + sides
    weights += [fetch(weight, 2, 1) for weight in weights]
    (going_right, going_left), grads = tied((going_right, going_left), grads)
    chunks += [going_right, going_left]
    edges = shift(going_right[3 * BLOCK:], 1)
    center = shift(going_left[:3 * BLOCK], -1)
    total, last_weight = project_most(table, weights, chunks)
    low_out, high_out = project_edge(last_weight, total, edges)
    outer_low_out = lax.ppermute(high_out, "dp", up)
    outer_high_out = lax.ppermute(low_out, "dp", down)
    projected = project_center(table, last_weight, total, center, low_out, high_out)
    projected = finish(table, outer_low_out, outer_high_out, projected)
    return (projected, *grads)


def solution(mesh):
    placed = P("dp", "tensor")
    return jax.shard_map(
        body,
        mesh=mesh,
        in_specs=(placed, placed, placed, P(), P(), P("tensor", "dp"), placed),
        out_specs=(placed, placed, placed, placed),
        check_vma=False,
    )
```
